32 devices in a mesh: dp: 32 (over z, y, x, core).
Axes of the slice: x: 2, y: 2, z: 4, core: 2. Of those that a mesh axis runs over, the one named last changes fastest.
Arguments:
- image_pooled: bfloat16 [12288, 1152], P('dp'), may hold values from -24 to 24
- text_embed: bfloat16 [12288, 1152], P('dp'), may hold values from -40 to 40
- head_weight: bfloat16 [1152, 1152], replicated, may hold values from -1.4 to 1.4
- logit_scale: float32 [1], replicated, may hold values from 3 to 10
- logit_bias: float32 [1], replicated, may hold values from -2 to 1
Outputs:
- row_loss: float32 [12288], P('dp')
- text_grad: float32 [12288, 1152], P('dp')
- head_grad: float32 [1152, 1152], replicated
The draws below stay inside these ranges and needn't reach their ends.
All inputs are finite; a program needn't handle non-finite values.
Results may differ from the reference program's by a relative error of at most 0.0003.
Values may be sent and summed in bfloat16 or wider, within the bound.
A program may use at most 128 MiB of HBM per device.

```python
import math
import jax
import jax.numpy as jnp
from jax import lax

D = 1152
TOK_DEV = 384
STEPS = 4
TOKENS = 12288
N_DP = 32


def pooled_base(key, lift):
    first, second, third = jax.random.split(key, 3)
    common = jax.random.truncated_normal(first, -4.0, 4.0, (1, D), jnp.float32)
    noise = jax.random.truncated_normal(second, -4.0, 4.0, (TOKENS, D), jnp.float32)
    share = jax.random.uniform(third, (TOKENS, 1), jnp.float32, lift, lift + 0.6)
    return (noise + share * common, common)


def draw_image_pooled(key, part):
    lift = 0.1
    upper = 2.0
    image, common = pooled_base(key, lift)
    key = jax.random.fold_in(key, 11)
    scale = jnp.exp(jax.random.uniform(key, (TOKENS, 1), jnp.float32, math.log(0.5), math.log(upper)))
    return (image * scale).astype(jnp.bfloat16)


def draw_text_embed(key, part):
    lift = 0.1
    low = 0.3
    image, common = pooled_base(key, lift)
    key = jax.random.fold_in(key, 23)
    keys = jax.random.split(key, 5)
    own = jax.random.uniform(keys[0], (TOKENS, 1), jnp.float32, low, low + 0.55)
    shared = jax.random.uniform(keys[1], (TOKENS, 1), jnp.float32, 0.0, 0.4)
    hard = 0.8 * jax.random.uniform(keys[2], (TOKENS, 1), jnp.float32) ** 3
    noise = jax.random.truncated_normal(keys[3], -4.0, 4.0, (TOKENS, D), jnp.float32)
    scale = jnp.exp(jax.random.uniform(keys[4], (TOKENS, 1), jnp.float32, math.log(0.5), math.log(2.0)))
    neighbour = jnp.roll(image, -TOK_DEV, axis=0)
    text = own * image + shared * common + hard * neighbour + (1.0 - 0.5 * own) * noise
    return (text * scale).astype(jnp.bfloat16)


def draw_head_weight(key, part):
    key = jax.random.fold_in(key, 37)
    first, second = jax.random.split(key, 2)
    gain = jax.random.uniform(first, (1, D), jnp.float32, 0.7, 1.3)
    spread = jax.random.truncated_normal(second, -4.0, 4.0, (D, D), jnp.float32) * 0.7
    return (jnp.eye(D, dtype=jnp.float32) * gain + spread * D ** (-0.5)).astype(jnp.bfloat16)


def setup_inputs(seed: int = 0) -> dict:
    arg_keys = jax.random.split(jax.random.key(seed), 6)
    image_pooled = draw_image_pooled(jax.random.fold_in(arg_keys[5], 71), 0)
    text_embed = draw_text_embed(jax.random.fold_in(arg_keys[5], 71), 0)
    head_weight = draw_head_weight(jax.random.fold_in(arg_keys[5], 71), 0)
    logit_scale = jnp.clip(jax.random.uniform(arg_keys[3], (1,), jnp.float32, 3.0, 10.0), 3.0, 10.0)
    logit_bias = jnp.clip(jax.random.uniform(arg_keys[4], (1,), jnp.float32, -2.0, 1.0), -2.0, 1.0)
    return dict(image_pooled=image_pooled, text_embed=text_embed, head_weight=head_weight, logit_scale=logit_scale, logit_bias=logit_bias)


epsilon = 1e-06

def reference(image_pooled, text_embed, head_weight, logit_scale, logit_bias):
    projected = jnp.dot(image_pooled, head_weight, preferred_element_type=jnp.float32)
    inv_img = lax.rsqrt(lax.optimization_barrier(jnp.sum(projected * projected, axis=1, keepdims=True)) + epsilon)
    img_unit = projected * inv_img
    img_bf = img_unit.astype(jnp.bfloat16)
    text_float = text_embed.astype(jnp.float32)
    inv_txt = lax.rsqrt(lax.optimization_barrier(jnp.sum(text_float * text_float, axis=1, keepdims=True)) + epsilon)
    txt_unit = text_float * inv_txt
    txt_bf = txt_unit.astype(jnp.bfloat16)
    images = img_bf.astype(jnp.float32).reshape(N_DP, TOK_DEV, D)
    texts = txt_bf.astype(jnp.float32).reshape(N_DP, TOK_DEV, D)
    identity = jnp.eye(TOK_DEV, dtype=jnp.float32)
    temper = logit_scale[0]
    offset_bias = logit_bias[0]
    row_total = jnp.zeros((N_DP, TOK_DEV), jnp.float32)
    img_grad = jnp.zeros((N_DP, TOK_DEV, D), jnp.float32)
    unit_grad = jnp.zeros((N_DP, TOK_DEV, D), jnp.float32)
    high = lax.Precision.HIGHEST
    for offset in range(STEPS):
        txt_block = jnp.roll(texts, offset, axis=0)
        scores = jnp.einsum('nid,njd->nij', images, txt_block, precision=high)
        if offset == 0:
            target = 2.0 * identity - 1.0
        else:
            target = -jnp.ones_like(identity)
        logits = temper * scores + offset_bias
        row_total = row_total - lax.optimization_barrier(jnp.sum(jax.nn.log_sigmoid(target * logits), axis=2))
        coefficient = (-target * temper * jax.nn.sigmoid(-target * logits)).astype(jnp.bfloat16).astype(jnp.float32)
        img_grad = img_grad + jnp.einsum('nij,njd->nid', coefficient, txt_block, precision=high)
        back = jnp.einsum('nij,nid->njd', coefficient, images, precision=high)
        unit_grad = unit_grad + jnp.roll(back, -offset, axis=0)
    row_loss = (row_total / (STEPS * TOK_DEV)).reshape(TOKENS)
    unit_grad = unit_grad.reshape(TOKENS, D)
    img_grad = img_grad.reshape(TOKENS, D)
    text_grad = (unit_grad - txt_unit * lax.optimization_barrier(jnp.sum(txt_unit * unit_grad, axis=1, keepdims=True))) * inv_txt
    proj_grad = ((img_grad - img_unit * lax.optimization_barrier(jnp.sum(img_unit * img_grad, axis=1, keepdims=True))) * inv_img).astype(jnp.bfloat16)
    head_grad = jnp.dot(image_pooled.T, proj_grad, preferred_element_type=jnp.float32) / N_DP
    return (row_loss, text_grad, head_grad)
```

```python
import functools

import jax
import jax.numpy as jnp
from jax import lax
from jax.experimental import pallas as pl
from jax.experimental.pallas import tpu as pltpu
from jax.sharding import PartitionSpec as P

STEPS = 4
PARTS = 3
TILE = 8
LANES = 128


epsilon = 1e-06


def shifted(value, axis, steps):
    count = lax.axis_size(axis)
    pairs = [(source, (source + steps) % count) for source in range(count)]
    return lax.ppermute(value, axis, pairs)


def bit_orders(count):
    levels = count.bit_length() - 1
    middle = list(range(1, levels - 1))
    orders = []
    for part in range(PARTS):
        turn = part % max(len(middle), 1)
        orders.append([0] + middle[turn:] + middle[:turn] + [levels - 1])
    return orders


def bit_of(me, bit):
    return lax.rem(lax.div(me, 1 << bit), 2)


def partner_of(me, bit):
    return me + (1 - 2 * bit_of(me, bit)) * (1 << bit)


def greet(me, levels):
    barrier = pltpu.get_barrier_semaphore()
    for bit in range(levels):
        pl.semaphore_signal(
            barrier, inc=1, device_id=(partner_of(me, bit),), device_id_type=pl.DeviceIdType.MESH
        )
    pl.semaphore_wait(barrier, levels)


def sum_kernel(count, chunk, a_ref, g_ref, out_ref, total, landed, send_sem, recv_sem, back_send, back_recv):
    me = lax.axis_index("dp")
    orders = bit_orders(count)
    levels = count.bit_length() - 1
    width = a_ref.shape[1] // PARTS
    blocks = g_ref.shape[1] // LANES
    rows = width // TILE
    used = blocks * rows
    full = count * chunk
    greet(me, levels)

    def copy_at(part, step, start):
        half = full >> (step + 1)
        bit = orders[part][step]
        base = full - (full >> step)
        return pltpu.make_async_remote_copy(
            src_ref=total.at[part, pl.ds(start + (1 - bit_of(me, bit)) * half, half)],
            dst_ref=landed.at[part, pl.ds(base, half)],
            send_sem=send_sem.at[part, step],
            recv_sem=recv_sem.at[part, step],
            device_id=(partner_of(me, bit),),
            device_id_type=pl.DeviceIdType.MESH,
        )

    def add(part, where, source, length):
        size = chunk
        while size < 8 and length % (2 * size) == 0:
            size *= 2

        def body(i, carry):
            total[part, pl.ds(where + i * size, size)] += landed[part, pl.ds(source + i * size, size)]
            return carry

        lax.fori_loop(0, length // size, body, 0)

    copies = {}
    starts = [0] * PARTS
    for part in range(PARTS):
        product = lax.dot_general(
            a_ref[:, part * width:(part + 1) * width], g_ref[...],
            (((0,), (0,)), ((), ())), preferred_element_type=jnp.float32,
        )
        for block in range(blocks):
            total[part, pl.ds(block, rows, stride=blocks)] = product[
                :, block * LANES:(block + 1) * LANES
            ].reshape(rows, TILE, LANES)
        if full > used:
            total[part, used:] = jnp.zeros((full - used, TILE, LANES), jnp.float32)
        copies[part, 0] = copy_at(part, 0, 0)
        copies[part, 0].start()
    for step in range(levels):
        half = full >> (step + 1)
        base = full - (full >> step)
        for part in range(PARTS):
            copies[part, step].wait_recv()
            start = starts[part] + bit_of(me, orders[part][step]) * half
            starts[part] = start
            if step + 1 < levels:
                quarter = half // 2
                mine = bit_of(me, orders[part][step + 1])
                away, kept = (1 - mine) * quarter, mine * quarter
                add(part, start + away, base + away, quarter)
                copies[part, step + 1] = copy_at(part, step + 1, start)
                copies[part, step + 1].start()
                add(part, start + kept, base + kept, quarter)
            else:
                out_ref[part, pl.ds(start, half)] = (
                    total[part, pl.ds(start, half)] + landed[part, pl.ds(base, half)]
                ) * (1.0 / count)
    backs = {}
    for step in reversed(range(levels)):
        length = full >> (step + 1)
        for part in range(PARTS):
            if step + 1 < levels:
                backs[part, step + 1].wait_recv()
                bit = orders[part][step + 1]
                starts[part] = starts[part] - bit_of(me, bit) * (length // 2)
            where = out_ref.at[part, pl.ds(starts[part], length)]
            backs[part, step] = pltpu.make_async_remote_copy(
                src_ref=where,
                dst_ref=where,
                send_sem=back_send.at[part, step],
                recv_sem=back_recv.at[part, step],
                device_id=(partner_of(me, orders[part][step]),),
                device_id_type=pl.DeviceIdType.MESH,
            )
            backs[part, step].start()
    for part in range(PARTS):
        backs[part, 0].wait_recv()
    for copy in copies.values():
        copy.wait_send()
    for copy in backs.values():
        copy.wait_send()


def summed_head(image_pooled, proj_grad):
    count = lax.axis_size("dp")
    levels = count.bit_length() - 1
    depth, width = image_pooled.shape[1], proj_grad.shape[1]
    used = depth * width // (PARTS * TILE * LANES)
    chunk = -(-used // count)
    full = chunk * count
    vmem = pl.BlockSpec(memory_space=pltpu.VMEM)
    every = pl.pallas_call(
        functools.partial(sum_kernel, count, chunk),
        out_shape=jax.ShapeDtypeStruct((PARTS, full, TILE, LANES), jnp.float32),
        in_specs=[vmem, vmem],
        out_specs=vmem,
        scratch_shapes=[
            pltpu.VMEM((PARTS, full, TILE, LANES), jnp.float32),
            pltpu.VMEM((PARTS, full, TILE, LANES), jnp.float32),
            pltpu.SemaphoreType.DMA((PARTS, levels)),
            pltpu.SemaphoreType.DMA((PARTS, levels)),
            pltpu.SemaphoreType.DMA((PARTS, levels)),
            pltpu.SemaphoreType.DMA((PARTS, levels)),
        ],
        compiler_params=pltpu.CompilerParams(
            collective_id=0, has_side_effects=True, vmem_limit_bytes=40 * 1024 * 1024
        ),
        name="head_sum",
    )(image_pooled, proj_grad)
    values = every[:, :used].reshape(depth // TILE, width // LANES, TILE, LANES)
    return values.transpose(0, 2, 1, 3).reshape(depth, width)


def shards(image_pooled, text_embed, head_weight, logit_scale, logit_bias):
    projected = jnp.dot(image_pooled, head_weight, preferred_element_type=jnp.float32)
    inv_img = lax.rsqrt(jnp.sum(projected * projected, axis=1, keepdims=True) + epsilon)
    img_unit = projected * inv_img
    img_bf = img_unit.astype(jnp.bfloat16)
    text_float = text_embed.astype(jnp.float32)
    inv_txt = lax.rsqrt(jnp.sum(text_float * text_float, axis=1, keepdims=True) + epsilon)
    txt_unit = text_float * inv_txt
    txt_bf = txt_unit.astype(jnp.bfloat16)
    local_rows = image_pooled.shape[0]
    identity = jnp.eye(local_rows, dtype=jnp.float32)
    temper = logit_scale[0]
    offset_bias = logit_bias[0]

    def pair_block(images, texts, target):
        scores = lax.dot_general(
            images, texts, (((1,), (1,)), ((), ())), preferred_element_type=jnp.float32
        )
        logits = temper * scores + offset_bias
        loss_part = -jnp.sum(jax.nn.log_sigmoid(target * logits), axis=1)
        coefficient = (-target * temper * jax.nn.sigmoid(-target * logits)).astype(jnp.bfloat16)
        return (loss_part, coefficient)

    def text_side(coefficient, images):
        return lax.dot_general(
            coefficient, images, (((0,), (0,)), ((), ())), preferred_element_type=jnp.float32
        )

    txt_block = txt_bf
    img_block = img_bf
    row_total = jnp.zeros((local_rows,), jnp.float32)
    img_grad = jnp.zeros(img_unit.shape, jnp.float32)
    unit_grad = None
    for offset in range(STEPS):
        if offset > 0:
            txt_block = shifted(txt_block, "dp", 1)
            img_block = shifted(img_block, "dp", -1)
        if offset == 0:
            target = 2.0 * identity - 1.0
        else:
            target = -jnp.ones_like(identity)
        loss_part, coefficient = pair_block(img_bf, txt_block, target)
        row_total = row_total + loss_part
        img_grad = img_grad + jnp.dot(coefficient, txt_block, preferred_element_type=jnp.float32)
        if offset == 0:
            unit_grad = text_side(coefficient, img_bf)
        else:
            mirrored = pair_block(img_block, txt_bf, target)[1]
            unit_grad = unit_grad + text_side(mirrored, img_block)
    row_loss = row_total / (STEPS * local_rows)
    text_grad = (
        unit_grad - txt_unit * jnp.sum(txt_unit * unit_grad, axis=1, keepdims=True)
    ) * inv_txt
    proj_grad = (
        (img_grad - img_unit * jnp.sum(img_unit * img_grad, axis=1, keepdims=True)) * inv_img
    ).astype(jnp.bfloat16)
    head_grad = summed_head(image_pooled, proj_grad)
    return (row_loss, text_grad, head_grad)


def solution(mesh):
    in_specs = (P("dp", None), P("dp", None), P(), P(), P())
    out_specs = (P("dp"), P("dp", None), P())
    return jax.shard_map(shards, mesh=mesh, in_specs=in_specs, out_specs=out_specs, check_vma=False)
```

```python
import functools

import jax
import jax.numpy as jnp
from jax import lax
from jax.experimental import pallas as pl
from jax.experimental.pallas import tpu as pltpu
from jax.sharding import PartitionSpec as P

STEPS = 4
PARTS = 3
TILE = 8
LANES = 128


epsilon = 1e-06


def bit_orders(count):
    levels = count.bit_length() - 1
    middle = list(range(1, levels - 1))
    orders = []
    for part in range(PARTS):
        turn = part % max(len(middle), 1)
        orders.append([0] + middle[turn:] + middle[:turn] + [levels - 1])
    return orders


def bit_of(me, bit):
    return lax.rem(lax.div(me, 1 << bit), 2)


def partner_of(me, bit):
    return me + (1 - 2 * bit_of(me, bit)) * (1 << bit)


def kernel(
    count, chunk, scale_ref, bias_ref, a_ref, t_ref, w_ref,
    loss_ref, tg_ref, out_ref,
    txt_bf, img_bf, img_unit, inv_t, inv_i, img_grad, unit_grad, g_ref, txt_in, img_in,
    total, landed,
    txt_send, txt_recv, img_send, img_recv, send_sem, recv_sem, back_send, back_recv,
):
    me = lax.axis_index("dp")
    orders = bit_orders(count)
    levels = count.bit_length() - 1
    local_rows = a_ref.shape[0]
    width = a_ref.shape[1] // PARTS
    blocks = g_ref.shape[1] // LANES
    rows = width // TILE
    used = blocks * rows
    full = count * chunk
    temper = scale_ref[0]
    offset_bias = bias_ref[0]

    odd = lax.rem(me, 2)
    mate = me + 1 - 2 * odd
    ahead = lax.rem(me + 2, count)
    behind = lax.rem(me + count - 2, count)
    far = lax.rem(me + count - 3 + 6 * odd, count)
    text_third = mate * (1 - odd) + far * odd
    image_third = mate * odd + far * (1 - odd)

    barrier = pltpu.get_barrier_semaphore()
    peers = [partner_of(me, bit) for bit in range(levels)] + [ahead, behind, far]
    for peer in peers:
        pl.semaphore_signal(
            barrier, inc=1, device_id=(peer,), device_id_type=pl.DeviceIdType.MESH
        )

    def remote(source, target, send, recv, device):
        return pltpu.make_async_remote_copy(
            src_ref=source, dst_ref=target, send_sem=send, recv_sem=recv,
            device_id=(device,), device_id_type=pl.DeviceIdType.MESH,
        )

    text_float = t_ref[...].astype(jnp.float32)
    inverse = lax.rsqrt(jnp.sum(text_float * text_float, axis=1, keepdims=True) + epsilon)
    inv_t[...] = inverse
    txt_bf[...] = (text_float * inverse).astype(jnp.bfloat16)
    pl.semaphore_wait(barrier, len(peers))

    text_copies = [
        remote(txt_bf, txt_in.at[0], txt_send.at[0], txt_recv.at[0], ahead),
        remote(txt_bf, txt_in.at[1], txt_send.at[1], txt_recv.at[1], text_third),
        remote(txt_in.at[0], txt_in.at[2], txt_send.at[2], txt_recv.at[2], mate),
    ]
    image_copies = [
        remote(img_bf, img_in.at[0], img_send.at[0], img_recv.at[0], behind),
        remote(img_bf, img_in.at[1], img_send.at[1], img_recv.at[1], image_third),
        remote(img_in.at[0], img_in.at[2], img_send.at[2], img_recv.at[2], mate),
    ]
    text_copies[0].start()
    text_copies[1].start()

    projected = jnp.dot(a_ref[...], w_ref[...], preferred_element_type=jnp.float32)
    inverse = lax.rsqrt(jnp.sum(projected * projected, axis=1, keepdims=True) + epsilon)
    inv_i[...] = inverse
    img_unit[...] = projected * inverse
    img_bf[...] = img_unit[...].astype(jnp.bfloat16)

    def scored(left, right):
        scores = lax.dot_general(
            left, right, (((1,), (1,)), ((), ())), preferred_element_type=jnp.float32
        )
        return temper * scores + offset_bias

    def sigmoid_of(value):
        small = jnp.exp(-jnp.abs(value))
        share = 1.0 / (1.0 + small)
        return small, jnp.where(value >= 0.0, share, small * share)

    def image_side(texts, own):
        logits = scored(img_bf[...], texts[...])
        if own:
            where = lax.broadcasted_iota(jnp.int32, logits.shape, 0)
            same = where == lax.broadcasted_iota(jnp.int32, logits.shape, 1)
            target = jnp.where(same, 1.0, -1.0)
            opposed = -target * logits
            small, slope = sigmoid_of(opposed)
            coefficient = (-target * temper * slope).astype(jnp.bfloat16)
        else:
            opposed = logits
            small, slope = sigmoid_of(opposed)
            coefficient = (temper * slope).astype(jnp.bfloat16)
        part = jnp.sum(jnp.maximum(opposed, 0.0) + jnp.log1p(small), axis=1, keepdims=True)
        grad = jnp.dot(coefficient, texts[...], preferred_element_type=jnp.float32)
        if own:
            loss_ref[...] = part
            img_grad[...] = grad
            unit_grad[...] = lax.dot_general(
                coefficient, img_bf[...], (((0,), (0,)), ((), ())),
                preferred_element_type=jnp.float32,
            )
        else:
            loss_ref[...] += part
            img_grad[...] += grad

    def text_side(images):
        slope = sigmoid_of(scored(txt_bf[...], images[...]))[1]
        coefficient = (temper * slope).astype(jnp.bfloat16)
        unit_grad[...] += jnp.dot(coefficient, images[...], preferred_element_type=jnp.float32)

    image_side(txt_bf, True)
    text_copies[0].wait_recv()
    text_copies[2].start()
    image_side(txt_in.at[0], False)
    text_copies[1].wait_recv()
    image_copies[0].start()
    image_copies[1].start()
    image_side(txt_in.at[1], False)
    text_copies[2].wait_recv()
    image_side(txt_in.at[2], False)
    loss_ref[...] = loss_ref[...] / (STEPS * local_rows)
    inner = jnp.sum(img_unit[...] * img_grad[...], axis=1, keepdims=True)
    g_ref[...] = ((img_grad[...] - img_unit[...] * inner) * inv_i[...]).astype(jnp.bfloat16)

    def first_image():
        image_copies[0].wait_recv()
        image_copies[2].start()
        text_side(img_in.at[0])

    def second_image():
        image_copies[1].wait_recv()
        text_side(img_in.at[1])

    def third_image():
        image_copies[2].wait_recv()
        text_side(img_in.at[2])

    def finish_text():
        unit = t_ref[...].astype(jnp.float32) * inv_t[...]
        inner = jnp.sum(unit * unit_grad[...], axis=1, keepdims=True)
        tg_ref[...] = (unit_grad[...] - unit * inner) * inv_t[...]

    def copy_at(part, step, start):
        half = full >> (step + 1)
        bit = orders[part][step]
        base = full - (full >> step)
        return remote(
            total.at[part, pl.ds(start + (1 - bit_of(me, bit)) * half, half)],
            landed.at[part, pl.ds(base, half)],
            send_sem.at[part, step], recv_sem.at[part, step], partner_of(me, bit),
        )

    def add(part, where, source, length):
        size = chunk
        while size < 16 and length % (2 * size) == 0:
            size *= 2

        def body(i, carry):
            total[part, pl.ds(where + i * size, size)] += landed[part, pl.ds(source + i * size, size)]
            return carry

        lax.fori_loop(0, length // size, body, 0)

    copies = {}
    starts = [0] * PARTS
    for part in range(PARTS):
        product = lax.dot_general(
            a_ref[:, part * width:(part + 1) * width], g_ref[...],
            (((0,), (0,)), ((), ())), preferred_element_type=jnp.float32,
        )
        for block in range(blocks):
            total[part, pl.ds(block, rows, stride=blocks)] = product[
                :, block * LANES:(block + 1) * LANES
            ].reshape(rows, TILE, LANES)
        if full > used:
            total[part, used:] = jnp.zeros((full - used, TILE, LANES), jnp.float32)
        copies[part, 0] = copy_at(part, 0, 0)
        copies[part, 0].start()
    for step in range(levels):
        half = full >> (step + 1)
        base = full - (full >> step)
        for part in range(PARTS):
            copies[part, step].wait_recv()
            start = starts[part] + bit_of(me, orders[part][step]) * half
            starts[part] = start
            if step + 1 < levels:
                quarter = half // 2
                mine = bit_of(me, orders[part][step + 1])
                away, kept = (1 - mine) * quarter, mine * quarter
                add(part, start + away, base + away, quarter)
                copies[part, step + 1] = copy_at(part, step + 1, start)
                copies[part, step + 1].start()
                add(part, start + kept, base + kept, quarter)
            else:
                out_ref[part, pl.ds(start, half)] = (
                    total[part, pl.ds(start, half)] + landed[part, pl.ds(base, half)]
                ) * (1.0 / count)
        if step == 1:
            first_image()
    backs = {}
    for step in reversed(range(levels)):
        length = full >> (step + 1)
        for part in range(PARTS):
            if step + 1 < levels:
                backs[part, step + 1].wait_recv()
                bit = orders[part][step + 1]
                starts[part] = starts[part] - bit_of(me, bit) * (length // 2)
            where = out_ref.at[part, pl.ds(starts[part], length)]
            backs[part, step] = remote(
                where, where, back_send.at[part, step], back_recv.at[part, step],
                partner_of(me, orders[part][step]),
            )
            backs[part, step].start()
        if step == 2:
            second_image()
        if step == 1:
            third_image()
        if step == 0:
            finish_text()
    for part in range(PARTS):
        backs[part, 0].wait_recv()
    for copy in text_copies + image_copies + list(copies.values()) + list(backs.values()):
        copy.wait_send()


def shards(image_pooled, text_embed, head_weight, logit_scale, logit_bias):
    count = lax.axis_size("dp")
    levels = count.bit_length() - 1
    local_rows, depth = image_pooled.shape
    width = head_weight.shape[1]
    used = depth * width // (PARTS * TILE * LANES)
    chunk = -(-used // count)
    full = chunk * count
    vmem = pl.BlockSpec(memory_space=pltpu.VMEM)
    smem = pl.BlockSpec(memory_space=pltpu.SMEM)
    loss, text_grad, every = pl.pallas_call(
        functools.partial(kernel, count, chunk),
        out_shape=(
            jax.ShapeDtypeStruct((local_rows, 1), jnp.float32),
            jax.ShapeDtypeStruct((local_rows, width), jnp.float32),
            jax.ShapeDtypeStruct((PARTS, full, TILE, LANES), jnp.float32),
        ),
        in_specs=[smem, smem, vmem, vmem, vmem],
        out_specs=(vmem, vmem, vmem),
        scratch_shapes=[
            pltpu.VMEM((local_rows, width), jnp.bfloat16),
            pltpu.VMEM((local_rows, width), jnp.bfloat16),
            pltpu.VMEM((local_rows, width), jnp.float32),
            pltpu.VMEM((local_rows, 1), jnp.float32),
            pltpu.VMEM((local_rows, 1), jnp.float32),
            pltpu.VMEM((local_rows, width), jnp.float32),
            pltpu.VMEM((local_rows, width), jnp.float32),
            pltpu.VMEM((local_rows, width), jnp.bfloat16),
            pltpu.VMEM((STEPS - 1, local_rows, width), jnp.bfloat16),
            pltpu.VMEM((STEPS - 1, local_rows, width), jnp.bfloat16),
            pltpu.VMEM((PARTS, full, TILE, LANES), jnp.float32),
            pltpu.VMEM((PARTS, full, TILE, LANES), jnp.float32),
        ] + [pltpu.SemaphoreType.DMA((STEPS - 1,))] * 4
        + [pltpu.SemaphoreType.DMA((PARTS, levels))] * 4,
        compiler_params=pltpu.CompilerParams(
            collective_id=0, has_side_effects=True, vmem_limit_bytes=56 * 1024 * 1024
        ),
        name="window_and_head",
    )(logit_scale, logit_bias, image_pooled, text_embed, head_weight)
    head = every[:, :used].reshape(depth // TILE, width // LANES, TILE, LANES)
    head = head.transpose(0, 2, 1, 3).reshape(depth, width)
    return (loss.reshape(local_rows), text_grad, head)


def solution(mesh):
    in_specs = (P("dp", None), P("dp", None), P(), P(), P())
    out_specs = (P("dp"), P("dp", None), P())
    return jax.shard_map(shards, mesh=mesh, in_specs=in_specs, out_specs=out_specs, check_vma=False)
```

```python
import functools

import jax
import jax.numpy as jnp
from jax import lax
from jax.experimental import pallas as pl
from jax.experimental.pallas import tpu as pltpu
from jax.sharding import PartitionSpec as P

STEPS = 4
PARTS = 3
TILE = 8
LANES = 128
PIECES = 4


epsilon = 1e-06


def bit_orders(count):
    levels = count.bit_length() - 1
    middle = list(range(1, levels - 1))
    orders = []
    for part in range(PARTS):
        turn = part % max(len(middle), 1)
        orders.append(middle[turn:] + middle[:turn] + [levels - 1])
    return orders


def bit_of(me, bit):
    return lax.rem(lax.div(me, 1 << bit), 2)


def partner_of(me, bit):
    return me + (1 - 2 * bit_of(me, bit)) * (1 << bit)


def kernel(
    count, chunk, scale_ref, bias_ref, a_ref, t_ref, w_ref,
    loss_ref, tg_ref, out_ref,
    txt_bf, img_bf, img_unit, inv_t, inv_i, img_grad, unit_grad, g_ref, txt_in, img_in,
    turned, turned_in, g_in, total, landed,
    txt_send, txt_recv, img_send, img_recv, pair_send, pair_recv,
    send_sem, recv_sem, back_send, back_recv, over_send, over_recv,
):
    me = lax.axis_index("dp")
    orders = bit_orders(count)
    bits = count.bit_length() - 1
    levels = bits - 1
    local_rows = a_ref.shape[0]
    width = a_ref.shape[1] // PARTS
    blocks = g_ref.shape[1] // LANES
    rows = width // 2 // TILE
    used = blocks * rows
    full = count // 2 * chunk
    temper = scale_ref[0]
    offset_bias = bias_ref[0]

    odd = lax.rem(me, 2)
    mate = me + 1 - 2 * odd
    ahead = lax.rem(me + 2, count)
    behind = lax.rem(me + count - 2, count)
    far = lax.rem(me + count - 3 + 6 * odd, count)
    text_third = mate * (1 - odd) + far * odd
    image_third = mate * odd + far * (1 - odd)

    barrier = pltpu.get_barrier_semaphore()
    peers = [partner_of(me, bit) for bit in range(bits)] + [ahead, behind, far]
    for peer in peers:
        pl.semaphore_signal(
            barrier, inc=1, device_id=(peer,), device_id_type=pl.DeviceIdType.MESH
        )

    def remote(source, target, send, recv, device):
        return pltpu.make_async_remote_copy(
            src_ref=source, dst_ref=target, send_sem=send, recv_sem=recv,
            device_id=(device,), device_id_type=pl.DeviceIdType.MESH,
        )

    text_float = t_ref[...].astype(jnp.float32)
    inverse = lax.rsqrt(jnp.sum(text_float * text_float, axis=1, keepdims=True) + epsilon)
    inv_t[...] = inverse
    txt_bf[...] = (text_float * inverse).astype(jnp.bfloat16)
    pl.semaphore_wait(barrier, len(peers))

    text_copies = [
        remote(txt_bf, txt_in.at[0], txt_send.at[0], txt_recv.at[0], ahead),
        remote(txt_bf, txt_in.at[1], txt_send.at[1], txt_recv.at[1], text_third),
        remote(txt_in.at[0], txt_in.at[2], txt_send.at[2], txt_recv.at[2], mate),
    ]
    image_copies = [
        remote(img_bf, img_in.at[0], img_send.at[0], img_recv.at[0], behind),
        remote(img_bf, img_in.at[1], img_send.at[1], img_recv.at[1], image_third),
        remote(img_in.at[0], img_in.at[2], img_send.at[2], img_recv.at[2], mate),
    ]
    text_copies[0].start()
    text_copies[1].start()
    for part in range(PARTS):
        columns = a_ref[:, part * width:(part + 1) * width]
        turned[part] = columns.T.reshape(2, width // 2, local_rows)
    pair_copies = [
        remote(turned.at[:, 1 - odd], turned_in, pair_send.at[0], pair_recv.at[0], mate),
        remote(g_ref, g_in, pair_send.at[1], pair_recv.at[1], mate),
    ]
    pair_copies[0].start()

    projected = jnp.dot(a_ref[...], w_ref[...], preferred_element_type=jnp.float32)
    inverse = lax.rsqrt(jnp.sum(projected * projected, axis=1, keepdims=True) + epsilon)
    inv_i[...] = inverse
    img_unit[...] = projected * inverse
    img_bf[...] = img_unit[...].astype(jnp.bfloat16)
    image_copies[0].start()
    image_copies[1].start()

    def scored(left, right):
        scores = lax.dot_general(
            left, right, (((1,), (1,)), ((), ())), preferred_element_type=jnp.float32
        )
        return temper * scores + offset_bias

    def sigmoid_of(value):
        small = jnp.exp(-jnp.abs(value))
        share = 1.0 / (1.0 + small)
        return small, jnp.where(value >= 0.0, share, small * share)

    def image_side(texts, own):
        logits = scored(img_bf[...], texts[...])
        if own:
            where = lax.broadcasted_iota(jnp.int32, logits.shape, 0)
            same = where == lax.broadcasted_iota(jnp.int32, logits.shape, 1)
            target = jnp.where(same, 1.0, -1.0)
            opposed = -target * logits
            small, slope = sigmoid_of(opposed)
            coefficient = (-target * temper * slope).astype(jnp.bfloat16)
        else:
            opposed = logits
            small, slope = sigmoid_of(opposed)
            coefficient = (temper * slope).astype(jnp.bfloat16)
        part = jnp.sum(jnp.maximum(opposed, 0.0) + jnp.log1p(small), axis=1, keepdims=True)
        grad = jnp.dot(coefficient, texts[...], preferred_element_type=jnp.float32)
        if own:
            loss_ref[...] = part
            img_grad[...] = grad
            unit_grad[...] = lax.dot_general(
                coefficient, img_bf[...], (((0,), (0,)), ((), ())),
                preferred_element_type=jnp.float32,
            )
        else:
            loss_ref[...] += part
            img_grad[...] += grad

    def text_side(images):
        slope = sigmoid_of(scored(txt_bf[...], images[...]))[1]
        coefficient = (temper * slope).astype(jnp.bfloat16)
        unit_grad[...] += jnp.dot(coefficient, images[...], preferred_element_type=jnp.float32)

    image_side(txt_bf, True)
    text_copies[0].wait_recv()
    text_copies[2].start()
    image_side(txt_in.at[0], False)
    text_copies[1].wait_recv()
    image_side(txt_in.at[1], False)
    text_copies[2].wait_recv()
    image_side(txt_in.at[2], False)
    loss_ref[...] = loss_ref[...] / (STEPS * local_rows)
    inner = jnp.sum(img_unit[...] * img_grad[...], axis=1, keepdims=True)
    g_ref[...] = ((img_grad[...] - img_unit[...] * inner) * inv_i[...]).astype(jnp.bfloat16)
    pair_copies[1].start()

    def first_image():
        image_copies[0].wait_recv()
        image_copies[2].start()
        text_side(img_in.at[0])

    def second_image():
        image_copies[1].wait_recv()
        text_side(img_in.at[1])

    def third_image():
        image_copies[2].wait_recv()
        text_side(img_in.at[2])

    def finish_text():
        unit = t_ref[...].astype(jnp.float32) * inv_t[...]
        inner = jnp.sum(unit * unit_grad[...], axis=1, keepdims=True)
        tg_ref[...] = (unit_grad[...] - unit * inner) * inv_t[...]

    def copy_at(part, step, start):
        half = full >> (step + 1)
        bit = orders[part][step]
        base = full - (full >> step)
        return remote(
            total.at[part, pl.ds(start + (1 - bit_of(me, bit)) * half, half)],
            landed.at[part, pl.ds(base, half)],
            send_sem.at[part, step], recv_sem.at[part, step], partner_of(me, bit),
        )

    def add(part, where, source, length):
        size = chunk
        while size < 16 and length % (2 * size) == 0:
            size *= 2

        def body(i, carry):
            total[part, pl.ds(where + i * size, size)] += landed[part, pl.ds(source + i * size, size)]
            return carry

        lax.fori_loop(0, length // size, body, 0)

    def spread(part, block, product):
        return product[:, block * LANES:(block + 1) * LANES].reshape(rows, TILE, LANES)

    for part in range(PARTS):
        product = jnp.dot(turned[part, odd], g_ref[...], preferred_element_type=jnp.float32)
        for block in range(blocks):
            total[part, pl.ds(block, rows, stride=blocks)] = spread(part, block, product)
        if full > used:
            total[part, used:] = jnp.zeros((full - used, TILE, LANES), jnp.float32)
    pair_copies[0].wait_recv()
    pair_copies[1].wait_recv()
    copies = {}
    starts = [0] * PARTS
    for part in range(PARTS):
        product = jnp.dot(turned_in[part], g_in[...], preferred_element_type=jnp.float32)
        for block in range(blocks):
            total[part, pl.ds(block, rows, stride=blocks)] += spread(part, block, product)
        copies[part, 0] = copy_at(part, 0, 0)
        copies[part, 0].start()
    first_image()
    for step in range(levels):
        half = full >> (step + 1)
        base = full - (full >> step)
        for part in range(PARTS):
            copies[part, step].wait_recv()
            start = starts[part] + bit_of(me, orders[part][step]) * half
            starts[part] = start
            if step + 1 < levels:
                quarter = half // 2
                mine = bit_of(me, orders[part][step + 1])
                away, kept = (1 - mine) * quarter, mine * quarter
                add(part, start + away, base + away, quarter)
                copies[part, step + 1] = copy_at(part, step + 1, start)
                copies[part, step + 1].start()
                add(part, start + kept, base + kept, quarter)
            else:
                out_ref[part, odd, pl.ds(start, half)] = (
                    total[part, pl.ds(start, half)] + landed[part, pl.ds(base, half)]
                ) * (1.0 / count)
        if step == 0:
            second_image()
        if step == 1:
            third_image()
    backs = {}
    overs = []

    def send_over(part, slot, start, length):
        where = out_ref.at[part, odd, pl.ds(start, length)]
        copy = remote(where, where, over_send.at[part, slot], over_recv.at[part, slot], mate)
        copy.start()
        overs.append(copy)

    for step in reversed(range(levels)):
        length = full >> (step + 1)
        pieces = PIECES if step == 0 and length % PIECES == 0 else 1
        piece = length // pieces
        for part in range(PARTS):
            start = starts[part]
            for i in range(pieces):
                where = out_ref.at[part, odd, pl.ds(start + i * piece, piece)]
                slot = i if step == 0 else step + PIECES - 1
                backs[part, step, i] = remote(
                    where, where, back_send.at[part, slot], back_recv.at[part, slot],
                    partner_of(me, orders[part][step]),
                )
                backs[part, step, i].start()
            if step + 1 == levels:
                send_over(part, levels + PIECES - 1, start, length)
        if step == 0:
            finish_text()
        for i in range(pieces):
            for part in range(PARTS):
                backs[part, step, i].wait_recv()
                bit = bit_of(me, orders[part][step])
                other = starts[part] + (1 - 2 * bit) * length
                slot = i if step == 0 else step + PIECES - 1
                send_over(part, slot, other + i * piece, piece)
        for part in range(PARTS):
            starts[part] = starts[part] - bit_of(me, orders[part][step]) * length
    for copy in overs:
        copy.wait_recv()
    for copy in (
        text_copies + image_copies + pair_copies
        + list(copies.values()) + list(backs.values()) + overs
    ):
        copy.wait_send()


def shards(image_pooled, text_embed, head_weight, logit_scale, logit_bias):
    count = lax.axis_size("dp")
    levels = count.bit_length() - 2
    local_rows, depth = image_pooled.shape
    width = head_weight.shape[1]
    used = depth * width // (PARTS * 2 * TILE * LANES)
    chunk = -(-used // (count // 2))
    full = chunk * (count // 2)
    vmem = pl.BlockSpec(memory_space=pltpu.VMEM)
    smem = pl.BlockSpec(memory_space=pltpu.SMEM)
    loss, text_grad, every = pl.pallas_call(
        functools.partial(kernel, count, chunk),
        out_shape=(
            jax.ShapeDtypeStruct((local_rows, 1), jnp.float32),
            jax.ShapeDtypeStruct((local_rows, width), jnp.float32),
            jax.ShapeDtypeStruct((PARTS, 2, full, TILE, LANES), jnp.float32),
        ),
        in_specs=[smem, smem, vmem, vmem, vmem],
        out_specs=(vmem, vmem, vmem),
        scratch_shapes=[
            pltpu.VMEM((local_rows, width), jnp.bfloat16),
            pltpu.VMEM((local_rows, width), jnp.bfloat16),
            pltpu.VMEM((local_rows, width), jnp.float32),
            pltpu.VMEM((local_rows, 1), jnp.float32),
            pltpu.VMEM((local_rows, 1), jnp.float32),
            pltpu.VMEM((local_rows, width), jnp.float32),
            pltpu.VMEM((local_rows, width), jnp.float32),
            pltpu.VMEM((local_rows, width), jnp.bfloat16),
            pltpu.VMEM((STEPS - 1, local_rows, width), jnp.bfloat16),
            pltpu.VMEM((STEPS - 1, local_rows, width), jnp.bfloat16),
            pltpu.VMEM((PARTS, 2, depth // PARTS // 2, local_rows), jnp.bfloat16),
            pltpu.VMEM((PARTS, depth // PARTS // 2, local_rows), jnp.bfloat16),
            pltpu.VMEM((local_rows, width), jnp.bfloat16),
            pltpu.VMEM((PARTS, full, TILE, LANES), jnp.float32),
            pltpu.VMEM((PARTS, full, TILE, LANES), jnp.float32),
        ] + [pltpu.SemaphoreType.DMA((STEPS - 1,))] * 4
        + [pltpu.SemaphoreType.DMA((2,))] * 2
        + [pltpu.SemaphoreType.DMA((PARTS, levels + PIECES))] * 6,
        compiler_params=pltpu.CompilerParams(
            collective_id=0, has_side_effects=True, vmem_limit_bytes=44 * 1024 * 1024
        ),
        name="window_and_head",
    )(logit_scale, logit_bias, image_pooled, text_embed, head_weight)
    head = every[:, :, :used].reshape(depth // TILE, width // LANES, TILE, LANES)
    head = head.transpose(0, 2, 1, 3).reshape(depth, width)
    return (loss.reshape(local_rows), text_grad, head)


def solution(mesh):
    in_specs = (P("dp", None), P("dp", None), P(), P(), P())
    out_specs = (P("dp"), P("dp", None), P())
    return jax.shard_map(shards, mesh=mesh, in_specs=in_specs, out_specs=out_specs, check_vma=False)
```

```python
import functools

import jax
import jax.numpy as jnp
from jax import lax
from jax.experimental import pallas as pl
from jax.experimental.pallas import tpu as pltpu
from jax.sharding import PartitionSpec as P

STEPS = 4
PARTS = 6
TILE = 8
LANES = 128
PIECES = 2


epsilon = 1e-06


def bit_orders(count):
    levels = count.bit_length() - 1
    middle = list(range(1, levels - 1))
    orders = []
    for part in range(PARTS):
        turn = part % max(len(middle), 1)
        orders.append(middle[turn:] + middle[:turn] + [levels - 1])
    return orders


def bit_of(me, bit):
    return lax.rem(lax.div(me, 1 << bit), 2)


def partner_of(me, bit):
    return me + (1 - 2 * bit_of(me, bit)) * (1 << bit)


def kernel(
    count, chunk, scale_ref, bias_ref, a_hbm, t_hbm, w_hbm,
    loss_ref, tg_ref, out_ref,
    a_ref, t_ref, w_ref, load_sem, txt_bf, img_bf, img_unit, inv_t, inv_i, img_grad, unit_grad, g_ref, txt_in, img_in,
    turned, turned_in, g_in, total, landed,
    txt_send, txt_recv, img_send, img_recv, pair_send, pair_recv,
    send_sem, recv_sem, back_send, back_recv, over_send, over_recv,
):
    loads = [
        pltpu.make_async_copy(source, target, load_sem.at[i])
        for i, (source, target) in enumerate(((t_hbm, t_ref), (a_hbm, a_ref), (w_hbm, w_ref)))
    ]
    for load in loads:
        load.start()
    me = lax.axis_index("dp")
    orders = bit_orders(count)
    bits = count.bit_length() - 1
    levels = bits - 1
    local_rows = a_ref.shape[0]
    width = a_ref.shape[1] // PARTS
    blocks = g_ref.shape[1] // LANES
    rows = width // 2 // TILE
    used = blocks * rows
    full = count // 2 * chunk
    temper = scale_ref[0]
    offset_bias = bias_ref[0]

    odd = lax.rem(me, 2)
    mate = me + 1 - 2 * odd
    ahead = lax.rem(me + 2, count)
    behind = lax.rem(me + count - 2, count)
    far = lax.rem(me + count - 3 + 6 * odd, count)
    text_third = mate * (1 - odd) + far * odd
    image_third = mate * odd + far * (1 - odd)

    barrier = pltpu.get_barrier_semaphore()
    peers = [partner_of(me, bit) for bit in range(bits)] + [ahead, behind, far]
    for peer in peers:
        pl.semaphore_signal(
            barrier, inc=1, device_id=(peer,), device_id_type=pl.DeviceIdType.MESH
        )

    def remote(source, target, send, recv, device):
        return pltpu.make_async_remote_copy(
            src_ref=source, dst_ref=target, send_sem=send, recv_sem=recv,
            device_id=(device,), device_id_type=pl.DeviceIdType.MESH,
        )

    loads[0].wait()
    text_float = t_ref[...].astype(jnp.float32)
    inverse = lax.rsqrt(jnp.sum(text_float * text_float, axis=1, keepdims=True) + epsilon)
    inv_t[...] = inverse
    txt_bf[...] = (text_float * inverse).astype(jnp.bfloat16)
    pl.semaphore_wait(barrier, len(peers))

    text_copies = [
        remote(txt_bf, txt_in.at[0], txt_send.at[0], txt_recv.at[0], ahead),
        remote(txt_bf, txt_in.at[1], txt_send.at[1], txt_recv.at[1], text_third),
        remote(txt_in.at[0], txt_in.at[2], txt_send.at[2], txt_recv.at[2], mate),
    ]
    image_copies = [
        remote(img_bf, img_in.at[0], img_send.at[0], img_recv.at[0], behind),
        remote(img_bf, img_in.at[1], img_send.at[1], img_recv.at[1], image_third),
        remote(img_in.at[0], img_in.at[2], img_send.at[2], img_recv.at[2], mate),
    ]
    text_copies[0].start()
    text_copies[1].start()
    loads[1].wait()
    for part in range(0, PARTS, 2):
        columns = a_ref[:, part * width:(part + 2) * width]
        turned[part:part + 2] = columns.T.reshape(2, 2, width // 2, local_rows)
    pair_copies = [
        remote(turned.at[:, 1 - odd], turned_in, pair_send.at[0], pair_recv.at[0], mate),
        remote(g_ref, g_in, pair_send.at[1], pair_recv.at[1], mate),
    ]
    pair_copies[0].start()

    loads[2].wait()
    projected = jnp.dot(a_ref[...], w_ref[...], preferred_element_type=jnp.float32)
    inverse = lax.rsqrt(jnp.sum(projected * projected, axis=1, keepdims=True) + epsilon)
    inv_i[...] = inverse
    img_unit[...] = projected * inverse
    img_bf[...] = img_unit[...].astype(jnp.bfloat16)
    image_copies[0].start()
    image_copies[1].start()

    def scored(left, right):
        scores = lax.dot_general(
            left, right, (((1,), (1,)), ((), ())), preferred_element_type=jnp.float32
        )
        return temper * scores + offset_bias

    def sigmoid_of(value):
        small = jnp.exp(-jnp.abs(value))
        share = 1.0 / (1.0 + small)
        return small, jnp.where(value >= 0.0, share, small * share)

    def image_side(texts, own):
        logits = scored(img_bf[...], texts[...])
        if own:
            where = lax.broadcasted_iota(jnp.int32, logits.shape, 0)
            same = where == lax.broadcasted_iota(jnp.int32, logits.shape, 1)
            target = jnp.where(same, 1.0, -1.0)
            opposed = -target * logits
            small, slope = sigmoid_of(opposed)
            coefficient = (-target * temper * slope).astype(jnp.bfloat16)
        else:
            opposed = logits
            small, slope = sigmoid_of(opposed)
            coefficient = (temper * slope).astype(jnp.bfloat16)
        part = jnp.sum(jnp.maximum(opposed, 0.0) + jnp.log1p(small), axis=1, keepdims=True)
        grad = jnp.dot(coefficient, texts[...], preferred_element_type=jnp.float32)
        if own:
            loss_ref[...] = part
            img_grad[...] = grad
            unit_grad[...] = lax.dot_general(
                coefficient, img_bf[...], (((0,), (0,)), ((), ())),
                preferred_element_type=jnp.float32,
            )
        else:
            loss_ref[...] += part
            img_grad[...] += grad

    def text_side(images):
        slope = sigmoid_of(scored(txt_bf[...], images[...]))[1]
        coefficient = (temper * slope).astype(jnp.bfloat16)
        unit_grad[...] += jnp.dot(coefficient, images[...], preferred_element_type=jnp.float32)

    image_side(txt_bf, True)
    text_copies[0].wait_recv()
    text_copies[2].start()
    image_side(txt_in.at[0], False)
    text_copies[1].wait_recv()
    image_side(txt_in.at[1], False)
    text_copies[2].wait_recv()
    image_side(txt_in.at[2], False)
    loss_ref[...] = loss_ref[...] / (STEPS * local_rows)
    inner = jnp.sum(img_unit[...] * img_grad[...], axis=1, keepdims=True)
    g_ref[...] = ((img_grad[...] - img_unit[...] * inner) * inv_i[...]).astype(jnp.bfloat16)
    pair_copies[1].start()

    def first_image():
        image_copies[0].wait_recv()
        image_copies[2].start()
        text_side(img_in.at[0])

    def second_image():
        image_copies[1].wait_recv()
        text_side(img_in.at[1])

    def third_image():
        image_copies[2].wait_recv()
        text_side(img_in.at[2])

    def finish_text():
        unit = t_ref[...].astype(jnp.float32) * inv_t[...]
        inner = jnp.sum(unit * unit_grad[...], axis=1, keepdims=True)
        tg_ref[...] = (unit_grad[...] - unit * inner) * inv_t[...]

    def copy_at(part, step, start):
        half = full >> (step + 1)
        bit = orders[part][step]
        base = full - (full >> step)
        return remote(
            total.at[part, pl.ds(start + (1 - bit_of(me, bit)) * half, half)],
            landed.at[part, pl.ds(base, half)],
            send_sem.at[part, step], recv_sem.at[part, step], partner_of(me, bit),
        )

    def add(part, where, source, length):
        size = chunk
        while size < 16 and length % (2 * size) == 0:
            size *= 2

        def body(i, carry):
            total[part, pl.ds(where + i * size, size)] += landed[part, pl.ds(source + i * size, size)]
            return carry

        lax.fori_loop(0, length // size, body, 0)

    def spread(part, block, product):
        return product[:, block * LANES:(block + 1) * LANES].reshape(rows, TILE, LANES)

    for part in range(PARTS):
        product = jnp.dot(turned[part, odd], g_ref[...], preferred_element_type=jnp.float32)
        for block in range(blocks):
            total[part, pl.ds(block, rows, stride=blocks)] = spread(part, block, product)
        if full > used:
            total[part, used:] = jnp.zeros((full - used, TILE, LANES), jnp.float32)
    pair_copies[0].wait_recv()
    pair_copies[1].wait_recv()
    copies = {}
    starts = [0] * PARTS
    for part in range(PARTS):
        product = jnp.dot(turned_in[part], g_in[...], preferred_element_type=jnp.float32)
        for block in range(blocks):
            total[part, pl.ds(block, rows, stride=blocks)] += spread(part, block, product)
        copies[part, 0] = copy_at(part, 0, 0)
        copies[part, 0].start()
    first_image()
    for step in range(levels):
        half = full >> (step + 1)
        base = full - (full >> step)
        for part in range(PARTS):
            copies[part, step].wait_recv()
            start = starts[part] + bit_of(me, orders[part][step]) * half
            starts[part] = start
            if step + 1 < levels:
                quarter = half // 2
                mine = bit_of(me, orders[part][step + 1])
                away, kept = (1 - mine) * quarter, mine * quarter
                add(part, start + away, base + away, quarter)
                copies[part, step + 1] = copy_at(part, step + 1, start)
                copies[part, step + 1].start()
                add(part, start + kept, base + kept, quarter)
            else:
                out_ref[part, odd, pl.ds(start, half)] = (
                    total[part, pl.ds(start, half)] + landed[part, pl.ds(base, half)]
                ) * (1.0 / count)
        if step == 0:
            second_image()
        if step == 1:
            third_image()
    backs = {}
    overs = []

    def send_over(part, slot, start, length):
        where = out_ref.at[part, odd, pl.ds(start, length)]
        copy = remote(where, where, over_send.at[part, slot], over_recv.at[part, slot], mate)
        copy.start()
        overs.append(copy)

    for step in reversed(range(levels)):
        length = full >> (step + 1)
        pieces = PIECES if step == 0 and length % PIECES == 0 else 1
        piece = length // pieces
        for part in range(PARTS):
            start = starts[part]
            for i in range(pieces):
                where = out_ref.at[part, odd, pl.ds(start + i * piece, piece)]
                slot = i if step == 0 else step + PIECES - 1
                backs[part, step, i] = remote(
                    where, where, back_send.at[part, slot], back_recv.at[part, slot],
                    partner_of(me, orders[part][step]),
                )
                backs[part, step, i].start()
            if step + 1 == levels:
                send_over(part, levels + PIECES - 1, start, length)
        if step == 0:
            finish_text()
        for i in range(pieces):
            for part in range(PARTS):
                backs[part, step, i].wait_recv()
                bit = bit_of(me, orders[part][step])
                other = starts[part] + (1 - 2 * bit) * length
                slot = i if step == 0 else step + PIECES - 1
                send_over(part, slot, other + i * piece, piece)
        for part in range(PARTS):
            starts[part] = starts[part] - bit_of(me, orders[part][step]) * length
    for copy in overs:
        copy.wait_recv()
    for copy in (
        text_copies + image_copies + pair_copies
        + list(copies.values()) + list(backs.values()) + overs
    ):
        copy.wait_send()


def shards(image_pooled, text_embed, head_weight, logit_scale, logit_bias):
    count = lax.axis_size("dp")
    levels = count.bit_length() - 2
    local_rows, depth = image_pooled.shape
    width = head_weight.shape[1]
    used = depth * width // (PARTS * 2 * TILE * LANES)
    chunk = -(-used // (count // 2))
    full = chunk * (count // 2)
    vmem = pl.BlockSpec(memory_space=pltpu.VMEM)
    hbm = pl.BlockSpec(memory_space=pltpu.HBM)
    smem = pl.BlockSpec(memory_space=pltpu.SMEM)
    loss, text_grad, every = pl.pallas_call(
        functools.partial(kernel, count, chunk),
        out_shape=(
            jax.ShapeDtypeStruct((local_rows, 1), jnp.float32),
            jax.ShapeDtypeStruct((local_rows, width), jnp.float32),
            jax.ShapeDtypeStruct((PARTS, 2, full, TILE, LANES), jnp.float32),
        ),
        in_specs=[smem, smem, hbm, hbm, hbm],
        out_specs=(vmem, vmem, vmem),
        scratch_shapes=[
            pltpu.VMEM((local_rows, depth), jnp.bfloat16),
            pltpu.VMEM((local_rows, width), jnp.bfloat16),
            pltpu.VMEM((depth, width), jnp.bfloat16),
            pltpu.SemaphoreType.DMA((3,)),
            pltpu.VMEM((local_rows, width), jnp.bfloat16),
            pltpu.VMEM((local_rows, width), jnp.bfloat16),
            pltpu.VMEM((local_rows, width), jnp.float32),
            pltpu.VMEM((local_rows, 1), jnp.float32),
            pltpu.VMEM((local_rows, 1), jnp.float32),
            pltpu.VMEM((local_rows, width), jnp.float32),
            pltpu.VMEM((local_rows, width), jnp.float32),
            pltpu.VMEM((local_rows, width), jnp.bfloat16),
            pltpu.VMEM((STEPS - 1, local_rows, width), jnp.bfloat16),
            pltpu.VMEM((STEPS - 1, local_rows, width), jnp.bfloat16),
            pltpu.VMEM((PARTS, 2, depth // PARTS // 2, local_rows), jnp.bfloat16),
            pltpu.VMEM((PARTS, depth // PARTS // 2, local_rows), jnp.bfloat16),
            pltpu.VMEM((local_rows, width), jnp.bfloat16),
            pltpu.VMEM((PARTS, full, TILE, LANES), jnp.float32),
            pltpu.VMEM((PARTS, full, TILE, LANES), jnp.float32),
        ] + [pltpu.SemaphoreType.DMA((STEPS - 1,))] * 4
        + [pltpu.SemaphoreType.DMA((2,))] * 2
        + [pltpu.SemaphoreType.DMA((PARTS, levels + PIECES))] * 6,
        compiler_params=pltpu.CompilerParams(
            collective_id=0, has_side_effects=True, vmem_limit_bytes=56 * 1024 * 1024
        ),
        name="window_and_head",
    )(logit_scale, logit_bias, image_pooled, text_embed, head_weight)
    head = every[:, :, :used].reshape(depth // TILE, width // LANES, TILE, LANES)
    head = head.transpose(0, 2, 1, 3).reshape(depth, width)
    return (loss.reshape(local_rows), text_grad, head)


def solution(mesh):
    in_specs = (P("dp", None), P("dp", None), P(), P(), P())
    out_specs = (P("dp"), P("dp", None), P())
    return jax.shard_map(shards, mesh=mesh, in_specs=in_specs, out_specs=out_specs, check_vma=False)
```
